512 devices in a mesh: dp: 64 (over y_hi, z, core), mp: 8 (over x, y_lo).
Axes of the slice: x: 4, y: 4 (y_hi: 2, y_lo: 2; y = y_hi * 2 + y_lo), z: 16, core: 2. Of those that a mesh axis runs over, the one named last changes fastest.
Arguments:
- tokens: bfloat16 [32768, 4096], P(('dp', 'mp')), may hold values from -6 to 6
- key_grad: bfloat16 [32768, 1024], P('dp', 'mp'), may hold values from -6 to 6
- key_weight: bfloat16 [4096, 1024], P(None, 'mp'), may hold values from -0.1875 to 0.1875
- momentum: bfloat16 [64, 4096, 1024], P('dp', None, 'mp'), may hold values from -4 to 4
- band_freqs: int32 [2, 16], replicated, may hold values from 0 to 31, as said below
Outputs:
- new_momentum: bfloat16 [64, 4096, 1024], P('dp', None, 'mp')
- update: bfloat16 [4096, 1024], P(None, 'mp')
- input_grad: bfloat16 [32768, 4096], P(('dp', 'mp'))
The draws below stay inside these ranges and needn't reach their ends.
Inputs may be any that keep to these rules, and one draw needn't show every extreme that they name: `band_freqs`: each row holds 16 distinct frequencies in increasing order, the first 0 and the last 31.
All inputs are finite; a program needn't handle non-finite values.
Results may differ from the reference program's by a relative error of at most 0.017.
Values may be sent and summed in bfloat16 or wider, within the bound.
A program may use at most 128 MiB of HBM per device.

```python
import math
import jax
import jax.numpy as jnp
from jax import lax

D_IN = 4096
KV_COLS = 1024
SPAN = 64
BAND = 16
TOK_DP = 512
TOKENS = 32768
REPLICAS = 64
N_DP = 64
N_MP = 8


def pick_freqs(key):
    interior = jax.random.permutation(key, SPAN // 2 - 2)[:BAND - 2] + 1
    chosen = jnp.concatenate([jnp.array([0, SPAN // 2 - 1], jnp.int32), interior.astype(jnp.int32)])
    return jnp.sort(chosen)


def draw_band_freqs(key, part):
    key = jax.random.fold_in(key, 1)
    first_key, second_key = jax.random.split(key)
    return jnp.stack([pick_freqs(first_key), pick_freqs(second_key)]).astype(jnp.int32)


def level_of(rng, extent, pieces, smallest, high):
    loudness, own = 1.0, jax.random.fold_in(rng, 6)
    for dim, parts in pieces:
        draws = jnp.exp(jax.random.uniform(jax.random.fold_in(own, dim), (parts,), jnp.float32, smallest / len(pieces), high / len(pieces)))
        loudness = loudness * jnp.repeat(draws, extent[dim] // parts).reshape([-1 if axis == dim else 1 for axis in range(len(extent))])
    return loudness


def gaussian(key, shape, deviation, reach, shards=(), kind=jnp.bfloat16):
    values = jax.random.normal(key, shape, jnp.float32) * deviation
    if len(shards) > 0:
        values = level_of(key, shape, shards, -0.22, 0.18) * values
    return jnp.clip(values, min=-reach, max=reach).astype(kind)


def setup_inputs(seed: int = 0) -> dict:
    key_list = jax.random.split(jax.random.key(seed), 6)
    return {
        "tokens": gaussian(key_list[0], (TOKENS, D_IN), 1.0, 6.0, ((0, 512),)),
        "key_grad": gaussian(key_list[1], (TOKENS, KV_COLS), 1.0, 6.0, ((0, 64), (1, 8))),
        "key_weight": gaussian(key_list[2], (D_IN, KV_COLS), KV_COLS ** -0.5, 0.1875, ((1, 8),)),
        "momentum": gaussian(key_list[3], (REPLICAS, D_IN, KV_COLS), 0.3, 4.0, ((0, 64), (2, 8))),
        "band_freqs": draw_band_freqs(jax.random.fold_in(key_list[5], 71), 0),
    }


momentum_decay = 0.999
exact_mode = lax.Precision.HIGHEST

def cosine_table(count):
    freq_idx = jnp.arange(count, dtype=jnp.float32)[:, None]
    cell_idx = jnp.arange(count, dtype=jnp.float32)[None, :]
    cosines = jnp.cos(math.pi * (2.0 * cell_idx + 1.0) * freq_idx / (2.0 * count))
    scales = jnp.where(freq_idx == 0.0, math.sqrt(1.0 / count), math.sqrt(2.0 / count))
    return (cosines * scales).astype(jnp.float32)

def pick_rows(cosines, freqs):
    selector = freqs[:, None] == jnp.arange(cosines.shape[0], dtype=jnp.int32)[None, :]
    return lax.optimization_barrier(jnp.sum(jnp.where(selector[:, :, None], cosines[None, :, :], jnp.float32(0.0)), axis=1))

def forward_band(moment, row_basis, col_basis):
    row_blocks = moment.shape[0] // SPAN
    col_blocks = moment.shape[1] // SPAN
    blocks = moment.reshape(row_blocks, SPAN, col_blocks, SPAN)
    left_done = jnp.einsum('ia,racb->ricb', row_basis, blocks, precision=exact_mode)
    return jnp.einsum('ricb,jb->ricj', left_done, col_basis, precision=exact_mode)

def inverse_band(band_coef, row_basis, col_basis):
    left_done = jnp.einsum('ricj,ia->racj', band_coef, row_basis, precision=exact_mode)
    blocks = jnp.einsum('racj,jb->racb', left_done, col_basis, precision=exact_mode)
    return blocks.reshape(blocks.shape[0] * SPAN, blocks.shape[2] * SPAN)

def reference(tokens, key_grad, key_weight, momentum, band_freqs):
    cosines = cosine_table(SPAN)
    row_basis = pick_rows(cosines, band_freqs[0])
    col_basis = pick_rows(cosines, band_freqs[1])

    def one_replica(inputs):
        tok_rows, key_rows, moment_in = inputs
        gradient = jnp.dot(tok_rows.T, key_rows, preferred_element_type=jnp.float32) / TOK_DP
        moment = momentum_decay * moment_in.astype(jnp.float32) + gradient
        band_coef = forward_band(moment, row_basis, col_basis)
        sent_band = lax.optimization_barrier(band_coef.astype(jnp.bfloat16))
        sent_float = sent_band.astype(jnp.float32)
        own_part = inverse_band(sent_float, row_basis, col_basis)
        return ((moment - own_part).astype(jnp.bfloat16), sent_float)
    new_momentum, sent_all = lax.map(one_replica, (tokens.reshape(N_DP, TOK_DP, D_IN), key_grad.reshape(N_DP, TOK_DP, KV_COLS), momentum))
    summed = lax.optimization_barrier(jnp.sum(sent_all, axis=0))
    update = inverse_band(summed, row_basis, col_basis).astype(jnp.bfloat16)
    local_cols = KV_COLS // N_MP
    total_grad = jnp.zeros((TOKENS, D_IN), jnp.float32)
    for head_group in range(N_MP):
        lower = head_group * local_cols
        partial_value = jnp.dot(key_grad[:, lower:lower + local_cols], key_weight[:, lower:lower + local_cols].T, preferred_element_type=jnp.float32)
        total_grad = total_grad + lax.optimization_barrier(partial_value.astype(jnp.bfloat16)).astype(jnp.float32)
    return (new_momentum, update, total_grad.astype(jnp.bfloat16))
```

```python
import functools
import math

import jax
import jax.numpy as jnp
import numpy as np
from jax import lax
from jax.experimental import pallas as pl
from jax.experimental.pallas import tpu as pltpu
from jax.sharding import PartitionSpec as P

MESH = pl.DeviceIdType.MESH
SPAN = 64
BAND = 16
DECAY = 0.999
N_X, N_Z = 4, 16
CHUNKS = 4
GROUP = 256
TOK = 64
BF = jnp.bfloat16
F32 = jnp.float32


def split(value):
    high = value.astype(BF)
    return high, (value - high.astype(F32)).astype(BF)


def mm(a, b, dims=((1,), (0,))):
    return lax.dot_general(a, b, (dims, ((), ())), preferred_element_type=F32)


def kernel(
    tok, kg, kw, mom, left_w, right_w, inv_right_w, inv_left_w,
    new_mom, update, in_grad,
    t_all, k_cat, k_rows, w_all, g_own, g_send, g_recv, c_send, s1, s2, s3, packed, p_own, p_send, p_recv,
    loc_sem, ks, kr, ts, tr, ws, wr, cs, cr, gs, gr, ps, pr, s1s, s1r, s2s, s2r, s3s, s3r, z_sem,
):
    width = t_all.shape[3]
    groups = width // GROUP
    dp, mp = lax.axis_index("dp"), lax.axis_index("mp")
    yh, z, core = dp // 32, (dp // 2) % N_Z, dp % 2
    x, yl = mp // 2, mp % 2
    part = yh * 2 + core

    def device(x=x, yl=yl, yh=yh, z=z, core=core):
        return (yh * 32 + z * 2 + core, x * 2 + yl)

    def x_at(step):
        return (x + N_X + step) % N_X

    def z_at(step):
        return (z + N_Z + step) % N_Z

    right, left, across = x_at(1), x_at(-1), x_at(2)
    sent = []

    def send(src, dst, send_sem, recv_sem, to):
        copy = pltpu.make_async_remote_copy(
            src_ref=src, dst_ref=dst, send_sem=send_sem, recv_sem=recv_sem, device_id=to, device_id_type=MESH
        )
        copy.start()
        sent.append(copy)
        return copy

    def lanes(i):
        return pl.ds(pl.multiple_of(i * 128, 128), 128)

    near = [device(x=right), device(x=left), device(x=across), device(z=z_at(1)), device(z=z_at(-1))]
    for o in range(1, 8):
        other = (yl * 4 + part + o) % 8
        near.append(device(yl=other // 4, yh=(other // 2) % 2, core=other % 2))
    barrier = pltpu.get_barrier_semaphore()
    for peer in near:
        pl.semaphore_signal(barrier, inc=1, device_id=peer, device_id_type=MESH)

    mine = pl.ds(pl.multiple_of(yl * TOK, TOK), TOK)
    theirs = pl.ds(pl.multiple_of((1 - yl) * TOK, TOK), TOK)
    local = [pltpu.make_async_copy(kg.at[:, mine], k_cat.at[:, :, pl.ds(0, 128)], loc_sem.at[0]),
             pltpu.make_async_copy(kg.at[x, mine], k_rows.at[0, :, lanes(x)], loc_sem.at[1]),
             pltpu.make_async_copy(kg.at[x, theirs], k_rows.at[1, :, lanes(x)], loc_sem.at[2]),
             pltpu.make_async_copy(kw, w_all.at[:, lanes(x)], loc_sem.at[3])]
    for c in range(CHUNKS):
        local.append(pltpu.make_async_copy(tok.at[:, pl.ds(c * width, width)], t_all.at[c, x], loc_sem.at[4 + c]))
    for copy in local:
        copy.start()
    pl.semaphore_wait(barrier, len(near))

    half = width // 2

    def token_piece(c, owner, rows=None):
        return t_all.at[c, owner] if rows is None else t_all.at[c, owner, rows]

    def weight_piece(c, owner, start=0, count=half):
        first = pl.multiple_of(c * width + core * half + start, 16)
        return w_all.at[pl.ds(first, count), lanes(owner)]

    def send_item(s):
        if s < CHUNKS:
            src, dst, ss, rs = tok.at[:, pl.ds(s * width, width)], token_piece(s, x), ts.at[s], tr.at[s]
        else:
            c = s - CHUNKS
            src = kw.at[pl.ds(pl.multiple_of(c * width + core * half, 16), half)]
            dst, ss, rs = weight_piece(c, x), ws.at[c], wr.at[c]
        return (send(src, dst, ss.at[0], rs.at[0], device(x=right)), send(src, dst, ss.at[1], rs.at[1], device(x=left)))

    def forward_item(s):
        if s < CHUNKS:
            lo, hi = pl.ds(0, TOK // 2), pl.ds(TOK // 2, TOK // 2)
            a, b = token_piece(s, left, lo), token_piece(s, right, hi)
            ss, rs = ts.at[s], tr.at[s]
        else:
            c = s - CHUNKS
            a, b = weight_piece(c, left, 0, half // 2), weight_piece(c, right, half // 2, half // 2)
            ss, rs = ws.at[c], wr.at[c]
        return (send(a, a, ss.at[2], rs.at[2], device(x=right)), send(b, b, ss.at[3], rs.at[3], device(x=left)))

    first_hop, second_hop, to_core = {}, {}, {}
    first_hop[0] = send_item(0)
    k_copies = [send(kg.at[:, theirs], k_cat.at[:, :, pl.ds(128, 128)], ks.at[0], kr.at[0], device(yl=1 - yl))]
    for i, other in enumerate((right, left, across)):
        k_copies.append(send(kg.at[other, mine], k_rows.at[0, :, lanes(x)], ks.at[1 + 2 * i], kr.at[1 + 2 * i], device(x=other)))
        k_copies.append(send(kg.at[other, theirs], k_rows.at[1, :, lanes(x)], ks.at[2 + 2 * i], kr.at[2 + 2 * i], device(x=other)))
    first_hop[1] = send_item(1)

    def z_round(r):
        for step in (1 << r, -(1 << r)):
            pl.semaphore_signal(z_sem.at[r], inc=1, device_id=device(z=z_at(step)), device_id_type=MESH)

    z_round(0)

    def left_band(block):
        columns = block.shape[1]
        high, low = split(block)
        both = mm(left_w[...], jnp.concatenate([high, low], axis=1))
        return both[:64, :columns] + both[:64, columns:] + both[64:, :columns]

    def right_band(rows):
        both = mm(packed[pl.ds(0, rows)], right_w[...])
        return (both[:, :128] + both[:, 128:]).astype(BF)

    def inverse(coef, g):
        both = mm(coef, inv_right_w[:, pl.ds(pl.multiple_of(g * GROUP, GROUP), GROUP)])
        high, low = split(both[:, :128] + both[:, 128:])
        return mm(inv_left_w[...], jnp.concatenate([high, low, high], axis=0))

    def group_rows(c, g):
        return pl.ds(pl.multiple_of(c * width + g * GROUP, GROUP), GROUP)

    def group_lanes(g):
        return pl.ds(pl.multiple_of(g * GROUP, GROUP), GROUP)

    g_copies, p_copies = {}, {}

    def gradient_chunk(c):
        def body(g, carry):
            t = t_all[c, :, :, group_lanes(g)].reshape(N_X * TOK, GROUP)
            grad = mm(t, k_cat[...].reshape(N_X * TOK, 256), ((0,), (0,))) * (1.0 / 512)
            rows = pl.ds(pl.multiple_of(g * GROUP, GROUP), GROUP)
            g_send[c, rows] = grad[:, 128:].astype(BF)
            own = grad[:, :128] + DECAY * mom[group_rows(c, g)].astype(F32)
            g_own[c, rows] = own
            y = left_band(jnp.concatenate([own, grad[:, 128:]], axis=1))
            high, low = split(jnp.concatenate([y[:, :128], y[:, 128:]], axis=0))
            packed[:, group_lanes(g)] = jnp.concatenate([high, low], axis=1)
            return carry

        lax.fori_loop(0, groups, body, 0)
        g_copies[c] = send(g_send.at[c], g_recv.at[c], gs.at[c], gr.at[c], device(yl=1 - yl))
        coef = right_band(128)
        c_send[c, 0] = coef[:64]
        c_send[c, 1] = coef[64:]
        slot = yl * 4 + part
        send(c_send.at[c, 1], s1.at[slot], s1s.at[c, 1], s1r.at[slot], device(yl=1 - yl, yh=c // 2, core=c % 2))

        @pl.when(part != c)
        def _():
            own_coef_copy(c).start()

        @pl.when(part == c)
        def _():
            s1[slot] = c_send[c, 0]

    def own_coef_copy(c):
        slot = yl * 4 + part
        return pltpu.make_async_remote_copy(
            src_ref=c_send.at[c, 0], dst_ref=s1.at[slot], send_sem=s1s.at[c, 0], recv_sem=s1r.at[slot],
            device_id=device(yh=c // 2, core=c % 2), device_id_type=MESH,
        )

    def s1_copy(o):
        slot = (yl * 4 + part + o) % 8
        return pltpu.make_async_remote_copy(
            src_ref=c_send.at[0, 0], dst_ref=s1.at[slot], send_sem=s1s.at[0, 0], recv_sem=s1r.at[slot],
            device_id=device(yl=1 - yl), device_id_type=MESH,
        )

    def s2_copy(o):
        return pltpu.make_async_remote_copy(
            src_ref=s2.at[z], dst_ref=s2.at[z], send_sem=s2s.at[o], recv_sem=s2r.at[z],
            device_id=device(z=(z + o) % N_Z), device_id_type=MESH,
        )

    def s2_arrival(o):
        other = (z + o) % N_Z
        return pltpu.make_async_remote_copy(
            src_ref=s2.at[z], dst_ref=s2.at[other], send_sem=s2s.at[o], recv_sem=s2r.at[other],
            device_id=device(z=other), device_id_type=MESH,
        )

    def s3_copy(o):
        other = (part + o) % 4
        return pltpu.make_async_remote_copy(
            src_ref=s3.at[part], dst_ref=s3.at[part], send_sem=s3s.at[o], recv_sem=s3r.at[part],
            device_id=device(yh=other // 2, core=other % 2), device_id_type=MESH,
        )

    def s3_arrival(o):
        other = (part + o) % 4
        return pltpu.make_async_remote_copy(
            src_ref=s3.at[part], dst_ref=s3.at[other], send_sem=s3s.at[o], recv_sem=s3r.at[other],
            device_id=device(yh=other // 2, core=other % 2), device_id_type=MESH,
        )

    def repeat(first, last, act):
        lax.fori_loop(first, last, lambda o, carry: (act(o), carry)[1], 0)

    def reduce_near(c):
        @pl.when(part == c)
        def _():
            repeat(1, 8, lambda o: s1_copy(o).wait_recv())
            total = s1[0].astype(F32)
            for i in range(1, 8):
                total = total + s1[i].astype(F32)
            s2[z] = total.astype(BF)
            repeat(1, N_Z, lambda o: s2_copy(o).start())

    def reduce_far(c):
        @pl.when(part == c)
        def _():
            repeat(1, N_Z, lambda o: s2_arrival(o).wait_recv())
            total = s2[0].astype(F32)
            for i in range(1, N_Z):
                total = total + s2[i].astype(F32)
            s3[part] = total.astype(BF)
            repeat(1, 4, lambda o: s3_copy(o).start())

    def momentum_chunk(c):
        g_copies[c].wait_recv()

        def forward(g, carry):
            rows = pl.ds(pl.multiple_of(g * GROUP, GROUP), GROUP)
            moment = g_own[c, rows] + g_recv[c, rows].astype(F32)
            g_own[c, rows] = moment
            high, low = split(left_band(moment))
            packed[pl.ds(0, 64), group_lanes(g)] = jnp.concatenate([high, low], axis=1)
            return carry

        lax.fori_loop(0, groups, forward, 0)
        c_send_own = right_band(64)

        def back(g, carry):
            rows = pl.ds(pl.multiple_of(g * GROUP, GROUP), GROUP)
            new_mom[group_rows(c, g)] = (g_own[c, rows] - inverse(c_send_own, g)).astype(BF)
            return carry

        lax.fori_loop(0, groups, back, 0)

    def partial_chunk(c):
        for copy in to_core[c]:
            copy.wait_recv()

        def body(g, carry):
            p = mm(k_rows[...].reshape(2 * TOK, 512), w_all[group_rows(c, g)], ((1,), (1,)))
            p_own[c, :, group_lanes(g)] = p[:TOK]
            p_send[c, :, group_lanes(g)] = p[TOK:].astype(BF)
            return carry

        lax.fori_loop(0, groups, body, 0)
        p_copies[c] = send(p_send.at[c], p_recv.at[c], ps.at[c], pr.at[c], device(yl=1 - yl))

    other_core = device(core=1 - core)
    for copy in local:
        copy.wait()

    for s in range(2 * CHUNKS + 2):
        if s < 2 * CHUNKS:
            for copy in first_hop[s]:
                copy.wait_recv()
            second_hop[s] = forward_item(s)
            if s + 2 < 2 * CHUNKS:
                first_hop[s + 2] = send_item(s + 2)
            if s >= CHUNKS:
                c = s - CHUNKS
                to_core[c] = []
                for i, owner in enumerate((left, right)):
                    piece = weight_piece(c, owner)
                    to_core[c].append(send(piece, piece, cs.at[c, i], cr.at[c, i], other_core))
        if 1 <= s <= 2 * CHUNKS:
            for copy in second_hop[s - 1]:
                copy.wait_recv()
            if s - 1 >= CHUNKS:
                c = s - 1 - CHUNKS
                piece = weight_piece(c, across)
                to_core[c].append(send(piece, piece, cs.at[c, 2], cr.at[c, 2], other_core))
        if s == 1:
            for copy in k_copies:
                copy.wait_recv()
        if s < 3:
            pl.semaphore_wait(z_sem.at[s], 2)
            if s < 2:
                z_round(s + 1)
        if 1 <= s <= CHUNKS:
            gradient_chunk(s - 1)
        if 2 <= s <= CHUNKS + 1:
            reduce_near(s - 2)
        if s >= CHUNKS + 2:
            partial_chunk(s - CHUNKS - 2)
        if CHUNKS + 1 <= s <= 2 * CHUNKS:
            reduce_far(s - CHUNKS - 1)
        if s in (3, 5, 6, 8):
            momentum_chunk({3: 0, 5: 1, 6: 2, 8: 3}[s])

    for c in range(CHUNKS):
        p_copies[c].wait_recv()
        in_grad[:, pl.ds(c * width, width)] = (p_own[c] + p_recv[c].astype(F32)).astype(BF)

    repeat(1, 4, lambda o: s3_arrival(o).wait_recv())

    def finish(i, carry):
        c, g = i // groups, i % groups
        update[group_rows(c, g)] = inverse(s3[c], g).astype(BF)
        return carry

    lax.fori_loop(0, CHUNKS * groups, finish, 0)

    for copy in sent:
        copy.wait_send()
    for c in range(CHUNKS):

        @pl.when(part != c)
        def _():
            own_coef_copy(c).wait_send()

    repeat(1, N_Z, lambda o: s2_copy(o).wait_send())
    repeat(1, 4, lambda o: s3_copy(o).wait_send())


def cosine_table():
    freq = np.arange(SPAN, dtype=np.float64)[:, None]
    cell = np.arange(SPAN, dtype=np.float64)[None, :]
    scale = np.where(freq == 0.0, math.sqrt(1.0 / SPAN), math.sqrt(2.0 / SPAN))
    return (np.cos(math.pi * (2.0 * cell + 1.0) * freq / (2.0 * SPAN)) * scale).astype(np.float32)


def repeat_diagonal(block, count):
    eye = jnp.eye(count, dtype=F32)
    return (eye[:, None, :, None] * block[None, :, None, :]).reshape(count * block.shape[0], count * block.shape[1])


def bases(band_freqs):
    chosen = band_freqs[:, :, None] == jnp.arange(SPAN, dtype=jnp.int32)[None, None, :]
    basis = jnp.sum(jnp.where(chosen[..., None], cosine_table()[None, None], F32(0.0)), axis=2)
    high = lax.reduce_precision(basis, 8, 7)
    low = lax.reduce_precision(basis - high, 8, 7)
    row_high, row_low = repeat_diagonal(high[0], 4), repeat_diagonal(low[0], 4)
    left_w = jnp.concatenate([row_high, row_low], axis=0)
    inv_left_w = jnp.concatenate([row_high.T, row_high.T, row_low.T], axis=1)
    col_high, col_low = repeat_diagonal(high[1], 2), repeat_diagonal(low[1], 2)
    inv_right_w = repeat_diagonal(jnp.concatenate([col_high, col_low], axis=1), 4)
    high_t, low_t = col_high.T, col_low.T
    right_w = jnp.concatenate(
        [
            repeat_diagonal(jnp.concatenate([high_t, high_t], axis=0), 4),
            repeat_diagonal(jnp.concatenate([low_t, jnp.zeros_like(low_t)], axis=0), 4),
        ],
        axis=1,
    )
    return [w.astype(BF) for w in (left_w, right_w, inv_right_w, inv_left_w)]


def per_device(tokens, key_grad, key_weight, momentum, band_freqs):
    d_in = tokens.shape[1]
    width = d_in // CHUNKS
    vmem = pl.BlockSpec(memory_space=pltpu.VMEM)
    hbm = pl.BlockSpec(memory_space=pl.ANY)
    dma = pltpu.SemaphoreType.DMA
    new_momentum, update, input_grad = pl.pallas_call(
        kernel,
        out_shape=(
            jax.ShapeDtypeStruct((d_in, 128), BF),
            jax.ShapeDtypeStruct((d_in, 128), BF),
            jax.ShapeDtypeStruct((TOK, d_in), BF),
        ),
        in_specs=[hbm, vmem, hbm, vmem, vmem, vmem, vmem, vmem],
        out_specs=(vmem, vmem, vmem),
        scratch_shapes=[
            pltpu.VMEM((CHUNKS, N_X, TOK, width), BF),
            pltpu.VMEM((N_X, TOK, 256), BF),
            pltpu.VMEM((2, TOK, 512), BF),
            pltpu.VMEM((d_in, 512), BF),
            pltpu.VMEM((CHUNKS, width, 128), F32),
            pltpu.VMEM((CHUNKS, width, 128), BF),
            pltpu.VMEM((CHUNKS, width, 128), BF),
            pltpu.VMEM((CHUNKS, 2, 64, 128), BF),
            pltpu.VMEM((8, 64, 128), BF),
            pltpu.VMEM((N_Z, 64, 128), BF),
            pltpu.VMEM((4, 64, 128), BF),
            pltpu.VMEM((128, 4 * GROUP), BF),
            pltpu.VMEM((CHUNKS, TOK, width), F32),
            pltpu.VMEM((CHUNKS, TOK, width), BF),
            pltpu.VMEM((CHUNKS, TOK, width), BF),
            dma((4 + CHUNKS,)),
            dma((7,)),
            dma((7,)),
            dma((CHUNKS, 4)),
            dma((CHUNKS, 4)),
            dma((CHUNKS, 4)),
            dma((CHUNKS, 4)),
            dma((CHUNKS, 3)),
            dma((CHUNKS, 3)),
            dma((CHUNKS,)),
            dma((CHUNKS,)),
            dma((CHUNKS,)),
            dma((CHUNKS,)),
            dma((CHUNKS, 2)),
            dma((8,)),
            dma((N_Z,)),
            dma((N_Z,)),
            dma((4,)),
            dma((4,)),
            pltpu.SemaphoreType.REGULAR((3,)),
        ],
        compiler_params=pltpu.CompilerParams(
            collective_id=0, has_side_effects=True, vmem_limit_bytes=48 << 20
        ),
        name="band_step",
    )(tokens, key_grad.reshape(N_X, 2 * TOK, 128), key_weight, momentum[0], *bases(band_freqs))
    return new_momentum[None], update, input_grad


def solution(mesh):
    placed = (P(("dp", "mp"), None), P("dp", "mp"), P(None, "mp"), P("dp", None, "mp"), P())
    return jax.shard_map(
        per_device,
        mesh=mesh,
        in_specs=placed,
        out_specs=(P("dp", None, "mp"), P(None, "mp"), P(("dp", "mp"), None)),
        check_vma=False,
    )
```

```python
import functools
import math

import jax
import jax.numpy as jnp
import numpy as np
from jax import lax
from jax.experimental import pallas as pl
from jax.experimental.pallas import tpu as pltpu
from jax.sharding import PartitionSpec as P

MESH = pl.DeviceIdType.MESH
SPAN = 64
BAND = 16
DECAY = 0.999
N_X, N_Z = 4, 16
CHUNKS = 4
GROUP = 256
TOK = 64
BF = jnp.bfloat16
F32 = jnp.float32


def split(value):
    high = value.astype(BF)
    return high, (value - high.astype(F32)).astype(BF)


def mm(a, b, dims=((1,), (0,))):
    return lax.dot_general(a, b, (dims, ((), ())), preferred_element_type=F32)


def kernel(
    tok, kg, kw, mom_hbm, freqs, cosines,
    new_mom_hbm, update_hbm, in_grad_hbm,
    new_mom, update, in_grad, mom, left_w, right_w, inv_right_w, inv_left_w,
    t_all, k_cat, k_rows, w_all, g_own, g_send, g_recv, c_send, s1, s2, s3, packed, p_own, p_send, p_recv,
    loc_sem, ks, kr, ts, tr, ws, wr, cs, cr, gs, gr, ps, pr, s1s, s1r, s2s, s2r, s3s, s3r, z_sem, out_sem,
):
    width = t_all.shape[3]
    groups = width // GROUP
    dp, mp = lax.axis_index("dp"), lax.axis_index("mp")
    yh, z, core = dp // 32, (dp // 2) % N_Z, dp % 2
    x, yl = mp // 2, mp % 2
    part = yh * 2 + core

    def device(x=x, yl=yl, yh=yh, z=z, core=core):
        return (yh * 32 + z * 2 + core, x * 2 + yl)

    def x_at(step):
        return (x + N_X + step) % N_X

    def z_at(step):
        return (z + N_Z + step) % N_Z

    right, left, across = x_at(1), x_at(-1), x_at(2)
    sent = []

    def send(src, dst, send_sem, recv_sem, to):
        copy = pltpu.make_async_remote_copy(
            src_ref=src, dst_ref=dst, send_sem=send_sem, recv_sem=recv_sem, device_id=to, device_id_type=MESH
        )
        copy.start()
        sent.append(copy)
        return copy

    def lanes(i):
        return pl.ds(pl.multiple_of(i * 128, 128), 128)

    near = [device(x=right), device(x=left), device(x=across), device(z=z_at(1)), device(z=z_at(-1))]
    for o in range(1, 8):
        other = (yl * 4 + part + o) % 8
        near.append(device(yl=other // 4, yh=(other // 2) % 2, core=other % 2))
    barrier = pltpu.get_barrier_semaphore()
    for peer in near:
        pl.semaphore_signal(barrier, inc=1, device_id=peer, device_id_type=MESH)

    mine = pl.ds(pl.multiple_of(yl * TOK, TOK), TOK)
    theirs = pl.ds(pl.multiple_of((1 - yl) * TOK, TOK), TOK)
    local = [pltpu.make_async_copy(kg.at[:, mine], k_cat.at[:, :, pl.ds(0, 128)], loc_sem.at[0]),
             pltpu.make_async_copy(kg.at[x, mine], k_rows.at[0, :, lanes(x)], loc_sem.at[1]),
             pltpu.make_async_copy(kg.at[x, theirs], k_rows.at[1, :, lanes(x)], loc_sem.at[2]),
             pltpu.make_async_copy(kw, w_all.at[:, lanes(x)], loc_sem.at[3]),
             pltpu.make_async_copy(mom_hbm, mom, loc_sem.at[4])]
    for c in range(CHUNKS):
        local.append(pltpu.make_async_copy(tok.at[:, pl.ds(c * width, width)], t_all.at[c, x], loc_sem.at[5 + c]))
    for copy in local:
        copy.start()
    pl.semaphore_wait(barrier, len(near))

    half = width // 2

    def token_piece(c, owner, rows=None):
        return t_all.at[c, owner] if rows is None else t_all.at[c, owner, rows]

    def weight_piece(c, owner, start=0, count=half):
        first = pl.multiple_of(c * width + core * half + start, 16)
        return w_all.at[pl.ds(first, count), lanes(owner)]

    def send_item(s):
        if s < CHUNKS:
            src, dst, ss, rs = tok.at[:, pl.ds(s * width, width)], token_piece(s, x), ts.at[s], tr.at[s]
        else:
            c = s - CHUNKS
            src = kw.at[pl.ds(pl.multiple_of(c * width + core * half, 16), half)]
            dst, ss, rs = weight_piece(c, x), ws.at[c], wr.at[c]
        return (send(src, dst, ss.at[0], rs.at[0], device(x=right)), send(src, dst, ss.at[1], rs.at[1], device(x=left)))

    def forward_item(s):
        if s < CHUNKS:
            lo, hi = pl.ds(0, TOK // 2), pl.ds(TOK // 2, TOK // 2)
            a, b = token_piece(s, left, lo), token_piece(s, right, hi)
            ss, rs = ts.at[s], tr.at[s]
        else:
            c = s - CHUNKS
            a, b = weight_piece(c, left, 0, half // 2), weight_piece(c, right, half // 2, half // 2)
            ss, rs = ws.at[c], wr.at[c]
        return (send(a, a, ss.at[2], rs.at[2], device(x=right)), send(b, b, ss.at[3], rs.at[3], device(x=left)))

    first_hop, second_hop, to_core = {}, {}, {}
    first_hop[0] = send_item(0)
    k_copies = [send(kg.at[:, theirs], k_cat.at[:, :, pl.ds(128, 128)], ks.at[0], kr.at[0], device(yl=1 - yl))]
    for i, other in enumerate((right, left, across)):
        k_copies.append(send(kg.at[other, mine], k_rows.at[0, :, lanes(x)], ks.at[1 + 2 * i], kr.at[1 + 2 * i], device(x=other)))
        k_copies.append(send(kg.at[other, theirs], k_rows.at[1, :, lanes(x)], ks.at[2 + 2 * i], kr.at[2 + 2 * i], device(x=other)))
    first_hop[1] = send_item(1)

    def basis_weights():
        def iota(shape, dim, shift, mask):
            return (lax.broadcasted_iota(jnp.int32, shape, dim) >> shift) & mask

        copies = iota((BAND, 128), 0, 0, 15) == iota((BAND, 128), 1, 0, 15)
        spread = mm(freqs[...].astype(F32).astype(BF), copies.astype(F32).astype(BF))
        freq = lax.broadcasted_iota(jnp.int32, (SPAN, 128), 0).astype(F32)
        row_hot, col_hot = [(freq == spread[i : i + 1]).astype(F32).astype(BF) for i in range(2)]
        high, low = cosines[0], cosines[1]
        over = ((0,), (0,))
        same = iota((64, 256), 0, 4, 3) == iota((64, 256), 1, 6, 3)
        for i, table in enumerate((high, low)):
            left_w[pl.ds(64 * i, 64)] = jnp.where(same, mm(row_hot, table, over)[:64], 0.0).astype(BF)
        same = iota((256, 128), 0, 6, 3) == iota((256, 128), 1, 4, 3)
        for i, table in enumerate((high, low)):
            inv_left_w[:, pl.ds(128 * i, 128)] = jnp.where(same, mm(table, row_hot, over), 0.0).astype(BF)
        both = mm(col_hot, jnp.concatenate([high[:, :128], low[:, :128]], axis=1), over)
        block = iota((128, 256), 0, 4, 1) == iota((128, 256), 1, 6, 1)
        for g in range(4):
            kept = block & (iota((128, 256), 0, 5, 3) == g)
            inv_right_w[:, pl.ds(GROUP * g, GROUP)] = jnp.where(kept, both, 0.0).astype(BF)
        block = iota((256, 128), 0, 6, 1) == iota((256, 128), 1, 4, 1)
        for i, table in enumerate((high, low)):
            one = mm(table, col_hot, over)
            for g in range(4):
                kept = block & (iota((256, 128), 1, 5, 3) == g)
                right_w[pl.ds(GROUP * g, GROUP), pl.ds(128 * i, 128)] = jnp.where(kept, one, 0.0).astype(BF)

    def z_round(r):
        for step in (1 << r, -(1 << r)):
            pl.semaphore_signal(z_sem.at[r], inc=1, device_id=device(z=z_at(step)), device_id_type=MESH)

    z_round(0)
    basis_weights()

    def left_band(block):
        columns = block.shape[1]
        high, low = split(block)
        both = mm(left_w[...], jnp.concatenate([high, low], axis=1))
        return both[:64, :columns] + both[:64, columns:] + both[64:, :columns]

    def right_band(rows):
        both = mm(packed[pl.ds(0, rows)], right_w[...])
        return (both[:, :128] + both[:, 128:]).astype(BF)

    def inverse(coef, g):
        both = mm(coef, inv_right_w[:, pl.ds(pl.multiple_of(g * GROUP, GROUP), GROUP)])
        high, low = split(both[:, :128] + both[:, 128:])
        return mm(inv_left_w[...], jnp.concatenate([high, low, high, low], axis=0))

    def group_rows(c, g):
        return pl.ds(pl.multiple_of(c * width + g * GROUP, GROUP), GROUP)

    def group_lanes(g):
        return pl.ds(pl.multiple_of(g * GROUP, GROUP), GROUP)

    g_copies, p_copies = {}, {}

    def gradient_chunk(c):
        def body(g, carry):
            t = t_all[c, :, :, group_lanes(g)].reshape(N_X * TOK, GROUP)
            grad = mm(t, k_cat[...].reshape(N_X * TOK, 256), ((0,), (0,))) * (1.0 / 512)
            rows = pl.ds(pl.multiple_of(g * GROUP, GROUP), GROUP)
            g_send[c, rows] = grad[:, 128:].astype(BF)
            own = grad[:, :128] + DECAY * mom[group_rows(c, g)].astype(F32)
            g_own[c, rows] = own
            y = left_band(jnp.concatenate([own, grad[:, 128:]], axis=1))
            high, low = split(jnp.concatenate([y[:, :128], y[:, 128:]], axis=0))
            packed[:, group_lanes(g)] = jnp.concatenate([high, low], axis=1)
            return carry

        lax.fori_loop(0, groups, body, 0, unroll=True)
        g_copies[c] = send(g_send.at[c], g_recv.at[c], gs.at[c], gr.at[c], device(yl=1 - yl))
        coef = right_band(128)
        c_send[c, 0] = coef[:64]
        c_send[c, 1] = coef[64:]
        s1[c, slot] = c_send[c, 0, pl.ds(pl.multiple_of(part * BAND, BAND), BAND)]
        repeat(1, 8, lambda o: s1_copy(c, o).start())

    slot = yl * 4 + part
    rows_of_part = pl.ds(pl.multiple_of(part * BAND, BAND), BAND)

    def repeat(first, last, act):
        lax.fori_loop(first, last, lambda o, carry: (act(o), carry)[1], 0)

    def remote(src, dst, send_sem, recv_sem, to):
        return pltpu.make_async_remote_copy(
            src_ref=src, dst_ref=dst, send_sem=send_sem, recv_sem=recv_sem, device_id=to, device_id_type=MESH
        )

    def s1_copy(c, o):
        to = (slot + o) % 8
        to_yl, to_part = to // 4, to % 4
        src = c_send.at[c, (to_yl + yl) % 2, pl.ds(pl.multiple_of(to_part * BAND, BAND), BAND)]
        to_device = device(yl=to_yl, yh=to_part // 2, core=to_part % 2)
        return remote(src, s1.at[c, slot], s1s.at[c], s1r.at[c], to_device)

    def s2_copy(c, o):
        return remote(s2.at[c, z], s2.at[c, z], s2s.at[c], s2r.at[c], device(z=(z + o) % N_Z))

    def s3_copy(c, o):
        to = (part + o) % 4
        piece = s3.at[c, rows_of_part]
        return remote(piece, piece, s3s.at[c], s3r.at[c], device(yh=to // 2, core=to % 2))

    def all_of(ref, send_sem, recv_sem):
        return remote(ref, ref, send_sem, recv_sem, device(core=1 - core))

    def s1_all(c):
        return all_of(s1.at[c, pl.ds(0, 7)], s1s.at[c], s1r.at[c])

    def s2_all(c):
        return all_of(s2.at[c, pl.ds(0, N_Z - 1)], s2s.at[c], s2r.at[c])

    def s3_all(c):
        return all_of(s3.at[c, pl.ds(0, 3 * BAND)], s3s.at[c], s3r.at[c])

    def reduce_near(c):
        s1_all(c).wait_recv()
        total = s1[c, 0].astype(F32)
        for i in range(1, 8):
            total = total + s1[c, i].astype(F32)
        s2[c, z] = total.astype(BF)
        repeat(1, N_Z, lambda o: s2_copy(c, o).start())

    def reduce_far(c):
        s2_all(c).wait_recv()
        total = s2[c, 0].astype(F32)
        for i in range(1, N_Z):
            total = total + s2[c, i].astype(F32)
        s3[c, rows_of_part] = total.astype(BF)
        repeat(1, 4, lambda o: s3_copy(c, o).start())

    written = []

    def write(i, c, src, dst):
        copy = pltpu.make_async_copy(src, dst, out_sem.at[i, c])
        copy.start()
        written.append(copy)

    def chunk_rows(c):
        return pl.ds(c * width, width)

    def update_chunk(c):
        s3_all(c).wait_recv()

        def body(g, carry):
            update[group_rows(c, g)] = inverse(s3[c], g).astype(BF)
            return carry

        lax.fori_loop(0, groups, body, 0, unroll=True)
        write(1, c, update.at[chunk_rows(c)], update_hbm.at[chunk_rows(c)])

    def momentum_chunk(c):
        g_copies[c].wait_recv()

        def forward(g, carry):
            rows = pl.ds(pl.multiple_of(g * GROUP, GROUP), GROUP)
            moment = g_own[c, rows] + g_recv[c, rows].astype(F32)
            g_own[c, rows] = moment
            high, low = split(left_band(moment))
            packed[pl.ds(0, 64), group_lanes(g)] = jnp.concatenate([high, low], axis=1)
            return carry

        lax.fori_loop(0, groups, forward, 0, unroll=True)
        c_send_own = right_band(64)

        def back(g, carry):
            rows = pl.ds(pl.multiple_of(g * GROUP, GROUP), GROUP)
            new_mom[group_rows(c, g)] = (g_own[c, rows] - inverse(c_send_own, g)).astype(BF)
            return carry

        lax.fori_loop(0, groups, back, 0, unroll=True)
        write(0, c, new_mom.at[chunk_rows(c)], new_mom_hbm.at[chunk_rows(c)])

    def partial_chunk(c):
        for copy in to_core[c]:
            copy.wait_recv()

        def body(g, carry):
            p = mm(k_rows[...].reshape(2 * TOK, 512), w_all[group_rows(c, g)], ((1,), (1,)))
            p_own[c, :, group_lanes(g)] = p[:TOK]
            p_send[c, :, group_lanes(g)] = p[TOK:].astype(BF)
            return carry

        lax.fori_loop(0, groups, body, 0, unroll=True)
        p_copies[c] = send(p_send.at[c], p_recv.at[c], ps.at[c], pr.at[c], device(yl=1 - yl))

    other_core = device(core=1 - core)
    for copy in local:
        copy.wait()

    for s in range(2 * CHUNKS + 2):
        if s < 2 * CHUNKS:
            for copy in first_hop[s]:
                copy.wait_recv()
            second_hop[s] = forward_item(s)
            if s + 2 < 2 * CHUNKS:
                first_hop[s + 2] = send_item(s + 2)
            if s >= CHUNKS:
                c = s - CHUNKS
                to_core[c] = []
                for i, owner in enumerate((left, right)):
                    piece = weight_piece(c, owner)
                    to_core[c].append(send(piece, piece, cs.at[c, i], cr.at[c, i], other_core))
        if 1 <= s <= 2 * CHUNKS:
            for copy in second_hop[s - 1]:
                copy.wait_recv()
            if s - 1 >= CHUNKS:
                c = s - 1 - CHUNKS
                piece = weight_piece(c, across)
                to_core[c].append(send(piece, piece, cs.at[c, 2], cr.at[c, 2], other_core))
        if s == 1:
            for copy in k_copies:
                copy.wait_recv()
        if s < 3:
            pl.semaphore_wait(z_sem.at[s], 2)
            if s < 2:
                z_round(s + 1)
        if 1 <= s <= CHUNKS:
            gradient_chunk(s - 1)
        if 2 <= s <= CHUNKS + 1:
            reduce_near(s - 2)
        if s >= CHUNKS + 2:
            partial_chunk(s - CHUNKS - 2)
        if CHUNKS + 1 <= s <= 2 * CHUNKS:
            reduce_far(s - CHUNKS - 1)
        if s in (4, 5, 6, 8):
            momentum_chunk({4: 0, 5: 1, 6: 2, 8: 3}[s])
        if s >= CHUNKS + 3:
            update_chunk(s - CHUNKS - 3)

    for c in range(CHUNKS):
        p_copies[c].wait_recv()
        in_grad[:, chunk_rows(c)] = (p_own[c] + p_recv[c].astype(F32)).astype(BF)
        write(2, c, in_grad.at[:, chunk_rows(c)], in_grad_hbm.at[:, chunk_rows(c)])

    update_chunk(CHUNKS - 1)

    for copy in written:
        copy.wait()
    for copy in sent:
        copy.wait_send()
    for c in range(CHUNKS):
        for copy in (s1_all(c), s2_all(c), s3_all(c)):
            copy.wait_send()


def hand_over(a, b, c, a_out, b_out, c_out, a_here, b_here, c_here, in_sem, out_sem):
    arrays = ((a, a_here, a_out), (b, b_here, b_out), (c, c_here, c_out))
    pieces = []
    for i, (src, here, dst) in enumerate(arrays):
        rows = src.shape[0] // 2
        for j in range(2):
            part = pl.ds(j * rows, rows)
            first = pltpu.make_async_copy(src.at[part], here.at[part], in_sem.at[i, j])
            second = pltpu.make_async_copy(here.at[part], dst.at[part], out_sem.at[i, j])
            first.start()
            pieces.append((first, second))
    for first, second in pieces:
        first.wait()
        second.start()
    for _, second in pieces:
        second.wait()


def cosine_table():
    freq = np.arange(SPAN, dtype=np.float64)[:, None]
    cell = np.arange(SPAN, dtype=np.float64)[None, :]
    scale = np.where(freq == 0.0, math.sqrt(1.0 / SPAN), math.sqrt(2.0 / SPAN))
    return (np.cos(math.pi * (2.0 * cell + 1.0) * freq / (2.0 * SPAN)) * scale).astype(np.float32)


def split_cosines():
    table = cosine_table()
    high = table.astype(BF)
    low = (table - high.astype(np.float32)).astype(BF)
    return np.stack([np.tile(high, (1, 4)), np.tile(low, (1, 4))])


def per_device(tokens, key_grad, key_weight, momentum, band_freqs):
    d_in = tokens.shape[1]
    width = d_in // CHUNKS
    vmem = pl.BlockSpec(memory_space=pltpu.VMEM)
    hbm = pl.BlockSpec(memory_space=pltpu.HBM)
    dma = pltpu.SemaphoreType.DMA
    new_momentum, update, input_grad = pl.pallas_call(
        kernel,
        out_shape=(
            jax.ShapeDtypeStruct((d_in, 128), BF),
            jax.ShapeDtypeStruct((d_in, 128), BF),
            jax.ShapeDtypeStruct((TOK, d_in), BF),
        ),
        in_specs=[hbm, hbm, hbm, hbm, vmem, vmem],
        out_specs=(hbm, hbm, hbm),
        scratch_shapes=[
            pltpu.VMEM((d_in, 128), BF),
            pltpu.VMEM((d_in, 128), BF),
            pltpu.VMEM((TOK, d_in), BF),
            pltpu.VMEM((d_in, 128), BF),
            pltpu.VMEM((128, GROUP), BF),
            pltpu.VMEM((4 * GROUP, 256), BF),
            pltpu.VMEM((128, 4 * GROUP), BF),
            pltpu.VMEM((GROUP, 256), BF),
            pltpu.VMEM((CHUNKS, N_X, TOK, width), BF),
            pltpu.VMEM((N_X, TOK, 256), BF),
            pltpu.VMEM((2, TOK, 512), BF),
            pltpu.VMEM((d_in, 512), BF),
            pltpu.VMEM((CHUNKS, width, 128), F32),
            pltpu.VMEM((CHUNKS, width, 128), BF),
            pltpu.VMEM((CHUNKS, width, 128), BF),
            pltpu.VMEM((CHUNKS, 2, 64, 128), BF),
            pltpu.VMEM((CHUNKS, 8, BAND, 128), BF),
            pltpu.VMEM((CHUNKS, N_Z, BAND, 128), BF),
            pltpu.VMEM((CHUNKS, 64, 128), BF),
            pltpu.VMEM((128, 4 * GROUP), BF),
            pltpu.VMEM((CHUNKS, TOK, width), F32),
            pltpu.VMEM((CHUNKS, TOK, width), BF),
            pltpu.VMEM((CHUNKS, TOK, width), BF),
            dma((5 + CHUNKS,)),
            dma((7,)),
            dma((7,)),
            dma((CHUNKS, 4)),
            dma((CHUNKS, 4)),
            dma((CHUNKS, 4)),
            dma((CHUNKS, 4)),
            dma((CHUNKS, 3)),
            dma((CHUNKS, 3)),
            dma((CHUNKS,)),
            dma((CHUNKS,)),
            dma((CHUNKS,)),
            dma((CHUNKS,)),
            dma((CHUNKS,)),
            dma((CHUNKS,)),
            dma((CHUNKS,)),
            dma((CHUNKS,)),
            dma((CHUNKS,)),
            dma((CHUNKS,)),
            pltpu.SemaphoreType.REGULAR((3,)),
            dma((3, CHUNKS)),
        ],
        compiler_params=pltpu.CompilerParams(
            collective_id=0, has_side_effects=True, vmem_limit_bytes=62 << 20
        ),
        name="band_step",
    )(tokens, key_grad.reshape(N_X, 2 * TOK, 128), key_weight, momentum[0], band_freqs, split_cosines())
    outs = (new_momentum, update, input_grad)
    new_momentum, update, input_grad = pl.pallas_call(
        hand_over,
        out_shape=tuple(jax.ShapeDtypeStruct(o.shape, o.dtype) for o in outs),
        in_specs=[pl.BlockSpec(memory_space=pl.ANY)] * 3,
        out_specs=(hbm,) * 3,
        scratch_shapes=[pltpu.VMEM(o.shape, o.dtype) for o in outs] + [dma((3, 2)), dma((3, 2))],
        name="hand_over",
    )(*outs)
    return new_momentum[None], update, input_grad


def solution(mesh):
    placed = (P(("dp", "mp"), None), P("dp", "mp"), P(None, "mp"), P("dp", None, "mp"), P())
    return jax.shard_map(
        per_device,
        mesh=mesh,
        in_specs=placed,
        out_specs=(P("dp", None, "mp"), P(None, "mp"), P(("dp", "mp"), None)),
        check_vma=False,
    )
```

```python
import functools
import math

import jax
import jax.numpy as jnp
import numpy as np
from jax import lax
from jax.experimental import pallas as pl
from jax.experimental.pallas import tpu as pltpu
from jax.sharding import PartitionSpec as P

MESH = pl.DeviceIdType.MESH
SPAN = 64
BAND = 16
DECAY = 0.999
N_X, N_Z = 4, 16
CHUNKS = 4
GROUP = 256
TOK = 64
BF = jnp.bfloat16
F32 = jnp.float32


def split(value):
    high = value.astype(BF)
    return high, (value - high.astype(F32)).astype(BF)


def mm(a, b, dims=((1,), (0,))):
    return lax.dot_general(a, b, (dims, ((), ())), preferred_element_type=F32)


def kernel(
    tok, kg, kw, mom_hbm, freqs, cosines,
    new_mom_hbm, update_hbm, in_grad_hbm,
    new_mom, update, in_grad, mom, left_w, right_w, inv_right_w, inv_left_w,
    t_all, k_cat, k_rows, w_all, g_own, g_send, g_recv, c_send, s1, s2, s3, packed, p_own, p_send, p_recv,
    loc_sem, ks, kr, ts, tr, ws, wr, cs, cr, gs, gr, ps, pr, s1s, s1r, s2s, s2r, s3s, s3r, z_sem, out_sem,
):
    width = t_all.shape[3]
    groups = width // GROUP
    dp, mp = lax.axis_index("dp"), lax.axis_index("mp")
    yh, z, core = dp // 32, (dp // 2) % N_Z, dp % 2
    x, yl = mp // 2, mp % 2
    part = yh * 2 + core

    def device(x=x, yl=yl, yh=yh, z=z, core=core):
        return (yh * 32 + z * 2 + core, x * 2 + yl)

    def x_at(step):
        return (x + N_X + step) % N_X

    def z_at(step):
        return (z + N_Z + step) % N_Z

    right, left, across = x_at(1), x_at(-1), x_at(2)
    sent = []

    def send(src, dst, send_sem, recv_sem, to):
        copy = pltpu.make_async_remote_copy(
            src_ref=src, dst_ref=dst, send_sem=send_sem, recv_sem=recv_sem, device_id=to, device_id_type=MESH
        )
        copy.start()
        sent.append(copy)
        return copy

    def lanes(i):
        return pl.ds(pl.multiple_of(i * 128, 128), 128)

    near = [device(x=right), device(x=left), device(x=across), device(z=z_at(1)), device(z=z_at(-1))]
    for o in range(1, 8):
        other = (yl * 4 + part + o) % 8
        near.append(device(yl=other // 4, yh=(other // 2) % 2, core=other % 2))
    barrier = pltpu.get_barrier_semaphore()
    for peer in near:
        pl.semaphore_signal(barrier, inc=1, device_id=peer, device_id_type=MESH)

    mine = pl.ds(pl.multiple_of(yl * TOK, TOK), TOK)
    theirs = pl.ds(pl.multiple_of((1 - yl) * TOK, TOK), TOK)
    local = [pltpu.make_async_copy(kg.at[:, mine], k_cat.at[:, :, pl.ds(0, 128)], loc_sem.at[0]),
             pltpu.make_async_copy(kg.at[x, mine], k_rows.at[0, :, lanes(x)], loc_sem.at[1]),
             pltpu.make_async_copy(kg.at[x, theirs], k_rows.at[1, :, lanes(x)], loc_sem.at[2]),
             pltpu.make_async_copy(kw, w_all.at[:, lanes(x)], loc_sem.at[3]),
             pltpu.make_async_copy(mom_hbm, mom, loc_sem.at[4])]
    for c in range(CHUNKS):
        local.append(pltpu.make_async_copy(tok.at[:, pl.ds(c * width, width)], t_all.at[c, x], loc_sem.at[5 + c]))
    for copy in local:
        copy.start()
    pl.semaphore_wait(barrier, len(near))

    half = width // 2

    def token_piece(c, owner, rows=None):
        return t_all.at[c, owner] if rows is None else t_all.at[c, owner, rows]

    def weight_piece(c, owner, start=0, count=half):
        first = pl.multiple_of(c * width + core * half + start, 16)
        return w_all.at[pl.ds(first, count), lanes(owner)]

    def send_item(s):
        if s < CHUNKS:
            src, dst, ss, rs = tok.at[:, pl.ds(s * width, width)], token_piece(s, x), ts.at[s], tr.at[s]
        else:
            c = s - CHUNKS
            src = kw.at[pl.ds(pl.multiple_of(c * width + core * half, 16), half)]
            dst, ss, rs = weight_piece(c, x), ws.at[c], wr.at[c]
        return (send(src, dst, ss.at[0], rs.at[0], device(x=right)), send(src, dst, ss.at[1], rs.at[1], device(x=left)))

    def forward_item(s):
        if s < CHUNKS:
            lo, hi = pl.ds(0, TOK // 2), pl.ds(TOK // 2, TOK // 2)
            a, b = token_piece(s, left, lo), token_piece(s, right, hi)
            ss, rs = ts.at[s], tr.at[s]
        else:
            c = s - CHUNKS
            a, b = weight_piece(c, left, 0, half // 2), weight_piece(c, right, half // 2, half // 2)
            ss, rs = ws.at[c], wr.at[c]
        return (send(a, a, ss.at[2], rs.at[2], device(x=right)), send(b, b, ss.at[3], rs.at[3], device(x=left)))

    first_hop, second_hop, to_core = {}, {}, {}
    first_hop[0] = send_item(0)
    k_copies = [send(kg.at[:, theirs], k_cat.at[:, :, pl.ds(128, 128)], ks.at[0], kr.at[0], device(yl=1 - yl))]
    for i, other in enumerate((right, left, across)):
        k_copies.append(send(kg.at[other, mine], k_rows.at[0, :, lanes(x)], ks.at[1 + 2 * i], kr.at[1 + 2 * i], device(x=other)))
        k_copies.append(send(kg.at[other, theirs], k_rows.at[1, :, lanes(x)], ks.at[2 + 2 * i], kr.at[2 + 2 * i], device(x=other)))
    first_hop[1] = send_item(1)

    def basis_weights():
        def iota(shape, dim, shift, mask):
            return (lax.broadcasted_iota(jnp.int32, shape, dim) >> shift) & mask

        copies = iota((BAND, 128), 0, 0, 15) == iota((BAND, 128), 1, 0, 15)
        spread = mm(freqs[...].astype(F32).astype(BF), copies.astype(F32).astype(BF))
        freq = lax.broadcasted_iota(jnp.int32, (SPAN, 128), 0).astype(F32)
        row_hot, col_hot = [(freq == spread[i : i + 1]).astype(F32).astype(BF) for i in range(2)]
        high, low = cosines[0], cosines[1]
        over = ((0,), (0,))
        same = iota((64, 256), 0, 4, 3) == iota((64, 256), 1, 6, 3)
        for i, table in enumerate((high, low)):
            left_w[pl.ds(64 * i, 64)] = jnp.where(same, mm(row_hot, table, over)[:64], 0.0).astype(BF)
        same = iota((256, 128), 0, 6, 3) == iota((256, 128), 1, 4, 3)
        for i, table in enumerate((high, low)):
            inv_left_w[:, pl.ds(128 * i, 128)] = jnp.where(same, mm(table, row_hot, over), 0.0).astype(BF)
        both = mm(col_hot, jnp.concatenate([high[:, :128], low[:, :128]], axis=1), over)
        block = iota((128, 256), 0, 4, 1) == iota((128, 256), 1, 6, 1)
        for g in range(4):
            kept = block & (iota((128, 256), 0, 5, 3) == g)
            inv_right_w[:, pl.ds(GROUP * g, GROUP)] = jnp.where(kept, both, 0.0).astype(BF)
        block = iota((256, 128), 0, 6, 1) == iota((256, 128), 1, 4, 1)
        for i, table in enumerate((high, low)):
            one = mm(table, col_hot, over)
            for g in range(4):
                kept = block & (iota((256, 128), 1, 5, 3) == g)
                right_w[pl.ds(GROUP * g, GROUP), pl.ds(128 * i, 128)] = jnp.where(kept, one, 0.0).astype(BF)

    def z_round(r):
        for step in (1 << r, -(1 << r)):
            pl.semaphore_signal(z_sem.at[r], inc=1, device_id=device(z=z_at(step)), device_id_type=MESH)

    z_round(0)
    basis_weights()

    def left_band(block):
        columns = block.shape[1]
        high, low = split(block)
        both = mm(left_w[...], jnp.concatenate([high, low], axis=1))
        return both[:64, :columns] + both[:64, columns:] + both[64:, :columns]

    def right_band(rows):
        both = mm(packed[pl.ds(0, rows)], right_w[...])
        return (both[:, :128] + both[:, 128:]).astype(BF)

    def inverse(coef, g):
        both = mm(coef, inv_right_w[:, pl.ds(pl.multiple_of(g * GROUP, GROUP), GROUP)])
        high, low = split(both[:, :128] + both[:, 128:])
        return mm(inv_left_w[...], jnp.concatenate([high, low, high, low], axis=0))

    def group_rows(c, g):
        return pl.ds(pl.multiple_of(c * width + g * GROUP, GROUP), GROUP)

    def group_lanes(g):
        return pl.ds(pl.multiple_of(g * GROUP, GROUP), GROUP)

    g_copies, p_copies = {}, {}

    def gradient_chunk(c):
        def body(g, carry):
            t = t_all[c, :, :, group_lanes(g)].reshape(N_X * TOK, GROUP)
            grad = mm(t, k_cat[...].reshape(N_X * TOK, 256), ((0,), (0,))) * (1.0 / 512)
            rows = pl.ds(pl.multiple_of(g * GROUP, GROUP), GROUP)
            g_send[c, rows] = grad[:, 128:].astype(BF)
            own = grad[:, :128] + DECAY * mom[group_rows(c, g)].astype(F32)
            g_own[c, rows] = own
            y = left_band(jnp.concatenate([own, grad[:, 128:]], axis=1))
            high, low = split(jnp.concatenate([y[:, :128], y[:, 128:]], axis=0))
            packed[:, group_lanes(g)] = jnp.concatenate([high, low], axis=1)
            return carry

        lax.fori_loop(0, groups, body, 0, unroll=True)
        coef = right_band(128)
        c_send[c, 0] = coef[:64]
        c_send[c, 1] = coef[64:]
        s1[c, slot] = c_send[c, 0, pl.ds(pl.multiple_of(part * BAND, BAND), BAND)]
        repeat(1, 8, lambda o: s1_copy(c, o).start())
        if c == CHUNKS - 1:
            send_gradient(c - 1, 1)
        send_gradient(c, 0)
        if c != CHUNKS - 2:
            send_gradient(c, 1)

    def send_gradient(c, i):
        rows = pl.ds(i * width // 2, width // 2)
        g_copies[c, i] = send(g_send.at[c, rows], g_recv.at[c, rows], gs.at[c, i], gr.at[c, i], device(yl=1 - yl))

    slot = yl * 4 + part
    rows_of_part = pl.ds(pl.multiple_of(part * BAND, BAND), BAND)

    def repeat(first, last, act):
        lax.fori_loop(first, last, lambda o, carry: (act(o), carry)[1], 0)

    def remote(src, dst, send_sem, recv_sem, to):
        return pltpu.make_async_remote_copy(
            src_ref=src, dst_ref=dst, send_sem=send_sem, recv_sem=recv_sem, device_id=to, device_id_type=MESH
        )

    def s1_copy(c, o):
        to = (slot + o) % 8
        to_yl, to_part = to // 4, to % 4
        src = c_send.at[c, (to_yl + yl) % 2, pl.ds(pl.multiple_of(to_part * BAND, BAND), BAND)]
        to_device = device(yl=to_yl, yh=to_part // 2, core=to_part % 2)
        return remote(src, s1.at[c, slot], s1s.at[c], s1r.at[c], to_device)

    def s2_copy(c, o):
        return remote(s2.at[c, z], s2.at[c, z], s2s.at[c], s2r.at[c], device(z=(z + o) % N_Z))

    def s3_copy(c, o):
        to = (part + o) % 4
        piece = s3.at[c, rows_of_part]
        return remote(piece, piece, s3s.at[c], s3r.at[c], device(yh=to // 2, core=to % 2))

    def all_of(ref, send_sem, recv_sem):
        return remote(ref, ref, send_sem, recv_sem, device(core=1 - core))

    def s1_all(c):
        return all_of(s1.at[c, pl.ds(0, 7)], s1s.at[c], s1r.at[c])

    def s2_all(c):
        return all_of(s2.at[c, pl.ds(0, N_Z - 1)], s2s.at[c], s2r.at[c])

    def s3_all(c):
        return all_of(s3.at[c, pl.ds(0, 3 * BAND)], s3s.at[c], s3r.at[c])

    def reduce_near(c):
        s1_all(c).wait_recv()
        total = s1[c, 0].astype(F32)
        for i in range(1, 8):
            total = total + s1[c, i].astype(F32)
        s2[c, z] = total.astype(BF)
        repeat(1, N_Z, lambda o: s2_copy(c, o).start())

    def reduce_far(c):
        s2_all(c).wait_recv()
        total = s2[c, 0].astype(F32)
        for i in range(1, N_Z):
            total = total + s2[c, i].astype(F32)
        s3[c, rows_of_part] = total.astype(BF)
        repeat(1, 4, lambda o: s3_copy(c, o).start())

    written = []

    def write(i, c, src, dst):
        copy = pltpu.make_async_copy(src, dst, out_sem.at[i, c])
        copy.start()
        written.append(copy)

    def chunk_rows(c):
        return pl.ds(c * width, width)

    def update_chunk(c):
        s3_all(c).wait_recv()

        def body(g, carry):
            update[group_rows(c, g)] = inverse(s3[c], g).astype(BF)
            return carry

        lax.fori_loop(0, groups, body, 0, unroll=True)
        write(1, c, update.at[chunk_rows(c)], update_hbm.at[chunk_rows(c)])

    def momentum_chunk(c):
        for i in range(2):
            g_copies[c, i].wait_recv()

        def forward(g, carry):
            rows = pl.ds(pl.multiple_of(g * GROUP, GROUP), GROUP)
            moment = g_own[c, rows] + g_recv[c, rows].astype(F32)
            g_own[c, rows] = moment
            high, low = split(left_band(moment))
            packed[pl.ds(0, 64), group_lanes(g)] = jnp.concatenate([high, low], axis=1)
            return carry

        lax.fori_loop(0, groups, forward, 0, unroll=True)
        c_send_own = right_band(64)

        def back(g, carry):
            rows = pl.ds(pl.multiple_of(g * GROUP, GROUP), GROUP)
            new_mom[group_rows(c, g)] = (g_own[c, rows] - inverse(c_send_own, g)).astype(BF)
            return carry

        lax.fori_loop(0, groups, back, 0, unroll=True)
        write(0, c, new_mom.at[chunk_rows(c)], new_mom_hbm.at[chunk_rows(c)])

    def partial_chunk(c):
        for copy in to_core[c]:
            copy.wait_recv()

        def body(g, carry):
            p = mm(k_rows[...].reshape(2 * TOK, 512), w_all[group_rows(c, g)], ((1,), (1,)))
            p_own[c, :, group_lanes(g)] = p[:TOK]
            p_send[c, :, group_lanes(g)] = p[TOK:].astype(BF)
            return carry

        lax.fori_loop(0, groups, body, 0, unroll=True)
        p_copies[c] = send(p_send.at[c], p_recv.at[c], ps.at[c], pr.at[c], device(yl=1 - yl))

    other_core = device(core=1 - core)
    for copy in local:
        copy.wait()

    for s in range(2 * CHUNKS + 2):
        if s < 2 * CHUNKS:
            for copy in first_hop[s]:
                copy.wait_recv()
            second_hop[s] = forward_item(s)
            if s + 2 < 2 * CHUNKS:
                first_hop[s + 2] = send_item(s + 2)
            if s >= CHUNKS:
                c = s - CHUNKS
                to_core[c] = []
                for i, owner in enumerate((left, right)):
                    piece = weight_piece(c, owner)
                    to_core[c].append(send(piece, piece, cs.at[c, i], cr.at[c, i], other_core))
        if 1 <= s <= 2 * CHUNKS:
            for copy in second_hop[s - 1]:
                copy.wait_recv()
            if s - 1 >= CHUNKS:
                c = s - 1 - CHUNKS
                piece = weight_piece(c, across)
                to_core[c].append(send(piece, piece, cs.at[c, 2], cr.at[c, 2], other_core))
        if s == 1:
            for copy in k_copies:
                copy.wait_recv()
        if s < 3:
            pl.semaphore_wait(z_sem.at[s], 2)
            if s < 2:
                z_round(s + 1)
        if 1 <= s <= CHUNKS:
            gradient_chunk(s - 1)
        if 2 <= s <= CHUNKS + 1:
            reduce_near(s - 2)
        if s >= CHUNKS + 2:
            partial_chunk(s - CHUNKS - 2)
        if CHUNKS + 1 <= s <= 2 * CHUNKS:
            reduce_far(s - CHUNKS - 1)
        if s in (4, 5, 6, 8):
            momentum_chunk({4: 0, 5: 1, 6: 2, 8: 3}[s])
        if s >= CHUNKS + 3:
            update_chunk(s - CHUNKS - 3)

    for c in range(CHUNKS):
        p_copies[c].wait_recv()
        in_grad[:, chunk_rows(c)] = (p_own[c] + p_recv[c].astype(F32)).astype(BF)
        write(2, c, in_grad.at[:, chunk_rows(c)], in_grad_hbm.at[:, chunk_rows(c)])

    update_chunk(CHUNKS - 1)

    for copy in written:
        copy.wait()
    for copy in sent:
        copy.wait_send()
    for c in range(CHUNKS):
        for copy in (s1_all(c), s2_all(c), s3_all(c)):
            copy.wait_send()


def hand_over(a, b, c, a_out, b_out, c_out, a_here, b_here, c_here, in_sem, out_sem):
    arrays = ((a, a_here, a_out), (b, b_here, b_out), (c, c_here, c_out))
    pieces = []
    for i, (src, here, dst) in enumerate(arrays):
        rows = src.shape[0] // 2
        for j in range(2):
            part = pl.ds(j * rows, rows)
            first = pltpu.make_async_copy(src.at[part], here.at[part], in_sem.at[i, j])
            second = pltpu.make_async_copy(here.at[part], dst.at[part], out_sem.at[i, j])
            first.start()
            pieces.append((first, second))
    for first, second in pieces:
        first.wait()
        second.start()
    for _, second in pieces:
        second.wait()


def cosine_table():
    freq = np.arange(SPAN, dtype=np.float64)[:, None]
    cell = np.arange(SPAN, dtype=np.float64)[None, :]
    scale = np.where(freq == 0.0, math.sqrt(1.0 / SPAN), math.sqrt(2.0 / SPAN))
    return (np.cos(math.pi * (2.0 * cell + 1.0) * freq / (2.0 * SPAN)) * scale).astype(np.float32)


def split_cosines():
    table = cosine_table()
    high = table.astype(BF)
    low = (table - high.astype(np.float32)).astype(BF)
    return np.stack([np.tile(high, (1, 4)), np.tile(low, (1, 4))])


def per_device(tokens, key_grad, key_weight, momentum, band_freqs):
    d_in = tokens.shape[1]
    width = d_in // CHUNKS
    vmem = pl.BlockSpec(memory_space=pltpu.VMEM)
    hbm = pl.BlockSpec(memory_space=pltpu.HBM)
    dma = pltpu.SemaphoreType.DMA
    new_momentum, update, input_grad = pl.pallas_call(
        kernel,
        out_shape=(
            jax.ShapeDtypeStruct((d_in, 128), BF),
            jax.ShapeDtypeStruct((d_in, 128), BF),
            jax.ShapeDtypeStruct((TOK, d_in), BF),
        ),
        in_specs=[hbm, hbm, hbm, hbm, vmem, vmem],
        out_specs=(hbm, hbm, hbm),
        scratch_shapes=[
            pltpu.VMEM((d_in, 128), BF),
            pltpu.VMEM((d_in, 128), BF),
            pltpu.VMEM((TOK, d_in), BF),
            pltpu.VMEM((d_in, 128), BF),
            pltpu.VMEM((128, GROUP), BF),
            pltpu.VMEM((4 * GROUP, 256), BF),
            pltpu.VMEM((128, 4 * GROUP), BF),
            pltpu.VMEM((GROUP, 256), BF),
            pltpu.VMEM((CHUNKS, N_X, TOK, width), BF),
            pltpu.VMEM((N_X, TOK, 256), BF),
            pltpu.VMEM((2, TOK, 512), BF),
            pltpu.VMEM((d_in, 512), BF),
            pltpu.VMEM((CHUNKS, width, 128), F32),
            pltpu.VMEM((CHUNKS, width, 128), BF),
            pltpu.VMEM((CHUNKS, width, 128), BF),
            pltpu.VMEM((CHUNKS, 2, 64, 128), BF),
            pltpu.VMEM((CHUNKS, 8, BAND, 128), BF),
            pltpu.VMEM((CHUNKS, N_Z, BAND, 128), BF),
            pltpu.VMEM((CHUNKS, 64, 128), BF),
            pltpu.VMEM((128, 4 * GROUP), BF),
            pltpu.VMEM((CHUNKS, TOK, width), F32),
            pltpu.VMEM((CHUNKS, TOK, width), BF),
            pltpu.VMEM((CHUNKS, TOK, width), BF),
            dma((5 + CHUNKS,)),
            dma((7,)),
            dma((7,)),
            dma((CHUNKS, 4)),
            dma((CHUNKS, 4)),
            dma((CHUNKS, 4)),
            dma((CHUNKS, 4)),
            dma((CHUNKS, 3)),
            dma((CHUNKS, 3)),
            dma((CHUNKS, 2)),
            dma((CHUNKS, 2)),
            dma((CHUNKS,)),
            dma((CHUNKS,)),
            dma((CHUNKS,)),
            dma((CHUNKS,)),
            dma((CHUNKS,)),
            dma((CHUNKS,)),
            dma((CHUNKS,)),
            dma((CHUNKS,)),
            pltpu.SemaphoreType.REGULAR((3,)),
            dma((3, CHUNKS)),
        ],
        compiler_params=pltpu.CompilerParams(
            collective_id=0, has_side_effects=True, vmem_limit_bytes=62 << 20
        ),
        name="band_step",
    )(tokens, key_grad.reshape(N_X, 2 * TOK, 128), key_weight, momentum[0], band_freqs, split_cosines())
    outs = (new_momentum, update, input_grad)
    new_momentum, update, input_grad = pl.pallas_call(
        hand_over,
        out_shape=tuple(jax.ShapeDtypeStruct(o.shape, o.dtype) for o in outs),
        in_specs=[pl.BlockSpec(memory_space=pl.ANY)] * 3,
        out_specs=(hbm,) * 3,
        scratch_shapes=[pltpu.VMEM(o.shape, o.dtype) for o in outs] + [dma((3, 2)), dma((3, 2))],
        name="hand_over",
    )(*outs)
    return new_momentum[None], update, input_grad


def solution(mesh):
    placed = (P(("dp", "mp"), None), P("dp", "mp"), P(None, "mp"), P("dp", None, "mp"), P())
    return jax.shard_map(
        per_device,
        mesh=mesh,
        in_specs=placed,
        out_specs=(P("dp", None, "mp"), P(None, "mp"), P(("dp", "mp"), None)),
        check_vma=False,
    )
```

```python
import functools
import math

import jax
import jax.numpy as jnp
import numpy as np
from jax import lax
from jax.experimental import pallas as pl
from jax.experimental.pallas import tpu as pltpu
from jax.sharding import PartitionSpec as P

MESH = pl.DeviceIdType.MESH
SPAN = 64
BAND = 16
DECAY = 0.999
N_X, N_Z = 4, 16
CHUNKS = 4
HALVES = 2 * CHUNKS
GROUP = 256
TOK = 64
BF = jnp.bfloat16
F32 = jnp.float32


LATE = (
    (("near", 2), ("mom", 1), ("near", 3)),
    (("far", 0),),
    (("far", 1), ("mom", 2)),
    (("far", 2), ("far", 3), ("upd", 0)),
    (("upd", 1), ("mom", 3)),
    (("upd", 2), ("upd", 3)),
)


def split(value):
    high = value.astype(BF)
    return high, (value - high.astype(F32)).astype(BF)


def mm(a, b, dims=((1,), (0,))):
    return lax.dot_general(a, b, (dims, ((), ())), preferred_element_type=F32)


def kernel(
    tok, kg, kw, mom_hbm, freqs, cosines,
    new_mom_hbm, update_hbm, in_grad_hbm,
    new_mom, update, in_grad, mom, left_w, right_w, inv_right_w, inv_left_w,
    t_all, k_cat, k_rows, w_all, g_own, g_send, g_recv, c_send, s1, s2, s3, packed, p_own, p_send, p_recv,
    loc_sem, ks, kr, ts, tr, ws, wr, cs, cr, gs, gr, ps, pr, s1s, s1r, s2s, s2r, s3s, s3r, z_sem, out_sem,
):
    width = 2 * t_all.shape[3]
    groups = width // GROUP
    dp, mp = lax.axis_index("dp"), lax.axis_index("mp")
    yh, z, core = dp // 32, (dp // 2) % N_Z, dp % 2
    x, yl = mp // 2, mp % 2
    part = yh * 2 + core

    def device(x=x, yl=yl, yh=yh, z=z, core=core):
        return (yh * 32 + z * 2 + core, x * 2 + yl)

    def x_at(step):
        return (x + N_X + step) % N_X

    def z_at(step):
        return (z + N_Z + step) % N_Z

    right, left, across = x_at(1), x_at(-1), x_at(2)
    sent = []

    def send(src, dst, send_sem, recv_sem, to):
        copy = pltpu.make_async_remote_copy(
            src_ref=src, dst_ref=dst, send_sem=send_sem, recv_sem=recv_sem, device_id=to, device_id_type=MESH
        )
        copy.start()
        sent.append(copy)
        return copy

    def lanes(i):
        return pl.ds(pl.multiple_of(i * 128, 128), 128)

    near = [device(x=right), device(x=left), device(x=across), device(z=z_at(1)), device(z=z_at(-1))]
    for o in range(1, 8):
        other = (yl * 4 + part + o) % 8
        near.append(device(yl=other // 4, yh=(other // 2) % 2, core=other % 2))
    barrier = pltpu.get_barrier_semaphore()
    for peer in near:
        pl.semaphore_signal(barrier, inc=1, device_id=peer, device_id_type=MESH)

    mine = pl.ds(pl.multiple_of(yl * TOK, TOK), TOK)
    theirs = pl.ds(pl.multiple_of((1 - yl) * TOK, TOK), TOK)
    local = [pltpu.make_async_copy(kg.at[:, mine], k_cat.at[:, :, pl.ds(0, 128)], loc_sem.at[0]),
             pltpu.make_async_copy(kg.at[x, mine], k_rows.at[0, :, lanes(x)], loc_sem.at[1]),
             pltpu.make_async_copy(kg.at[x, theirs], k_rows.at[1, :, lanes(x)], loc_sem.at[2]),
             pltpu.make_async_copy(kw, w_all.at[:, lanes(x)], loc_sem.at[3]),
             pltpu.make_async_copy(mom_hbm, mom, loc_sem.at[4])]
    half = width // 2
    for h in range(HALVES):
        local.append(pltpu.make_async_copy(tok.at[:, pl.ds(h * half, half)], t_all.at[h, x], loc_sem.at[5 + h]))
    for copy in local:
        copy.start()
    pl.semaphore_wait(barrier, len(near))


    def token_piece(c, owner, rows=None):
        return t_all.at[c, owner] if rows is None else t_all.at[c, owner, rows]

    def weight_piece(c, owner, start=0, count=half):
        first = pl.multiple_of(c * width + core * half + start, 16)
        return w_all.at[pl.ds(first, count), lanes(owner)]

    def send_item(s):
        if s < HALVES:
            src, dst, ss, rs = tok.at[:, pl.ds(s * half, half)], token_piece(s, x), ts.at[s], tr.at[s]
        else:
            c = s - HALVES
            src = kw.at[pl.ds(pl.multiple_of(c * width + core * half, 16), half)]
            dst, ss, rs = weight_piece(c, x), ws.at[c], wr.at[c]
        return (send(src, dst, ss.at[0], rs.at[0], device(x=right)), send(src, dst, ss.at[1], rs.at[1], device(x=left)))

    def forward_item(s):
        if s < HALVES:
            lo, hi = pl.ds(0, TOK // 2), pl.ds(TOK // 2, TOK // 2)
            a, b = token_piece(s, left, lo), token_piece(s, right, hi)
            ss, rs = ts.at[s], tr.at[s]
        else:
            c = s - HALVES
            a, b = weight_piece(c, left, 0, half // 2), weight_piece(c, right, half // 2, half // 2)
            ss, rs = ws.at[c], wr.at[c]
        return (send(a, a, ss.at[2], rs.at[2], device(x=right)), send(b, b, ss.at[3], rs.at[3], device(x=left)))

    first_hop, second_hop, to_core = {}, {}, {}
    first_hop[0] = send_item(0)
    k_copies = [send(kg.at[:, theirs], k_cat.at[:, :, pl.ds(128, 128)], ks.at[0], kr.at[0], device(yl=1 - yl))]
    for i, other in enumerate((right, left, across)):
        k_copies.append(send(kg.at[other, mine], k_rows.at[0, :, lanes(x)], ks.at[1 + 2 * i], kr.at[1 + 2 * i], device(x=other)))
        k_copies.append(send(kg.at[other, theirs], k_rows.at[1, :, lanes(x)], ks.at[2 + 2 * i], kr.at[2 + 2 * i], device(x=other)))
    first_hop[1] = send_item(1)
    first_hop[2] = send_item(2)

    def basis_weights():
        def iota(shape, dim, shift, mask):
            return (lax.broadcasted_iota(jnp.int32, shape, dim) >> shift) & mask

        copies = iota((BAND, 128), 0, 0, 15) == iota((BAND, 128), 1, 0, 15)
        spread = mm(freqs[...].astype(F32).astype(BF), copies.astype(F32).astype(BF))
        freq = lax.broadcasted_iota(jnp.int32, (SPAN, 128), 0).astype(F32)
        row_hot, col_hot = [(freq == spread[i : i + 1]).astype(F32).astype(BF) for i in range(2)]
        high, low = cosines[0], cosines[1]
        over = ((0,), (0,))
        same = iota((64, 256), 0, 4, 3) == iota((64, 256), 1, 6, 3)
        for i, table in enumerate((high, low)):
            left_w[pl.ds(64 * i, 64)] = jnp.where(same, mm(row_hot, table, over)[:64], 0.0).astype(BF)
        same = iota((256, 128), 0, 6, 3) == iota((256, 128), 1, 4, 3)
        for i, table in enumerate((high, low)):
            inv_left_w[:, pl.ds(128 * i, 128)] = jnp.where(same, mm(table, row_hot, over), 0.0).astype(BF)
        both = mm(col_hot, jnp.concatenate([high[:, :128], low[:, :128]], axis=1), over)
        block = iota((128, 256), 0, 4, 1) == iota((128, 256), 1, 6, 1)
        for g in range(4):
            kept = block & (iota((128, 256), 0, 5, 3) == g)
            inv_right_w[:, pl.ds(GROUP * g, GROUP)] = jnp.where(kept, both, 0.0).astype(BF)
        block = iota((256, 128), 0, 6, 1) == iota((256, 128), 1, 4, 1)
        for i, table in enumerate((high, low)):
            one = mm(table, col_hot, over)
            for g in range(4):
                kept = block & (iota((256, 128), 1, 5, 3) == g)
                right_w[pl.ds(GROUP * g, GROUP), pl.ds(128 * i, 128)] = jnp.where(kept, one, 0.0).astype(BF)

    def z_round(r):
        for step in (1 << r, -(1 << r)):
            pl.semaphore_signal(z_sem.at[r], inc=1, device_id=device(z=z_at(step)), device_id_type=MESH)

    z_round(0)
    basis_weights()

    def left_band(block):
        columns = block.shape[1]
        high, low = split(block)
        both = mm(left_w[...], jnp.concatenate([high, low], axis=1))
        return both[:64, :columns] + both[:64, columns:] + both[64:, :columns]

    def right_band(rows):
        both = mm(packed[pl.ds(0, rows)], right_w[...])
        return (both[:, :128] + both[:, 128:]).astype(BF)

    def inverse(coef, g):
        both = mm(coef, inv_right_w[:, pl.ds(pl.multiple_of(g * GROUP, GROUP), GROUP)])
        high, low = split(both[:, :128] + both[:, 128:])
        return mm(inv_left_w[...], jnp.concatenate([high, low, high, low], axis=0))

    def group_rows(c, g):
        return pl.ds(pl.multiple_of(c * width + g * GROUP, GROUP), GROUP)

    def group_lanes(g):
        return pl.ds(pl.multiple_of(g * GROUP, GROUP), GROUP)

    g_copies, p_copies = {}, {}

    def gradient_half(h):
        c = h // 2
        for i in range(groups // 2):
            g = (h % 2) * (groups // 2) + i
            t = t_all[h, :, :, group_lanes(i)].reshape(N_X * TOK, GROUP)
            grad = mm(t, k_cat[...].reshape(N_X * TOK, 256), ((0,), (0,))) * (1.0 / 512)
            rows = pl.ds(g * GROUP, GROUP)
            g_send[c, rows] = grad[:, 128:].astype(BF)
            own = grad[:, :128] + DECAY * mom[group_rows(c, g)].astype(F32)
            g_own[c, rows] = own
            y = left_band(jnp.concatenate([own, grad[:, 128:]], axis=1))
            high, low = split(jnp.concatenate([y[:, :128], y[:, 128:]], axis=0))
            packed[:, group_lanes(g)] = jnp.concatenate([high, low], axis=1)
        if h % 2 == 0:
            if h < HALVES - 2:
                send_gradient(c, 0)
            return
        coef = right_band(128)
        c_send[c, 0] = coef[:64]
        c_send[c, 1] = coef[64:]
        s1[c, slot] = c_send[c, 0, rows_of_part]
        repeat(1, 8, lambda o: s1_copy(c, o).start())
        if c == CHUNKS - 1:
            send_gradient(c - 1, 1)
            send_gradient(c, 0)
        if c != CHUNKS - 2:
            send_gradient(c, 1)

    def send_gradient(c, i):
        rows = pl.ds(i * width // 2, width // 2)
        g_copies[c, i] = send(g_send.at[c, rows], g_recv.at[c, rows], gs.at[c, i], gr.at[c, i], device(yl=1 - yl))

    slot = yl * 4 + part
    rows_of_part = pl.ds(pl.multiple_of(part * BAND, BAND), BAND)

    def repeat(first, last, act):
        lax.fori_loop(first, last, lambda o, carry: (act(o), carry)[1], 0)

    def remote(src, dst, send_sem, recv_sem, to):
        return pltpu.make_async_remote_copy(
            src_ref=src, dst_ref=dst, send_sem=send_sem, recv_sem=recv_sem, device_id=to, device_id_type=MESH
        )

    def s1_copy(c, o):
        to = (slot + o) % 8
        to_yl, to_part = to // 4, to % 4
        src = c_send.at[c, (to_yl + yl) % 2, pl.ds(pl.multiple_of(to_part * BAND, BAND), BAND)]
        to_device = device(yl=to_yl, yh=to_part // 2, core=to_part % 2)
        return remote(src, s1.at[c, slot], s1s.at[c], s1r.at[c], to_device)

    def s2_copy(c, o):
        return remote(s2.at[c, z], s2.at[c, z], s2s.at[c], s2r.at[c], device(z=(z + o) % N_Z))

    def s3_copy(c, o):
        to = (part + o) % 4
        piece = s3.at[c, rows_of_part]
        return remote(piece, piece, s3s.at[c], s3r.at[c], device(yh=to // 2, core=to % 2))

    def all_of(ref, send_sem, recv_sem):
        return remote(ref, ref, send_sem, recv_sem, device(core=1 - core))

    def s1_all(c):
        return all_of(s1.at[c, pl.ds(0, 7)], s1s.at[c], s1r.at[c])

    def s2_all(c):
        return all_of(s2.at[c, pl.ds(0, N_Z - 1)], s2s.at[c], s2r.at[c])

    def s3_all(c):
        return all_of(s3.at[c, pl.ds(0, 3 * BAND)], s3s.at[c], s3r.at[c])

    def reduce_near(c):
        s1_all(c).wait_recv()
        total = s1[c, 0].astype(F32)
        for i in range(1, 8):
            total = total + s1[c, i].astype(F32)
        s2[c, z] = total.astype(BF)
        repeat(1, N_Z, lambda o: s2_copy(c, o).start())

    def reduce_far(c):
        s2_all(c).wait_recv()
        total = s2[c, 0].astype(F32)
        for i in range(1, N_Z):
            total = total + s2[c, i].astype(F32)
        s3[c, rows_of_part] = total.astype(BF)
        repeat(1, 4, lambda o: s3_copy(c, o).start())

    written = []

    def write(i, c, src, dst):
        copy = pltpu.make_async_copy(src, dst, out_sem.at[i, c])
        copy.start()
        written.append(copy)

    def chunk_rows(c):
        return pl.ds(c * width, width)

    def update_chunk(c):
        s3_all(c).wait_recv()

        def body(g, carry):
            update[group_rows(c, g)] = inverse(s3[c], g).astype(BF)
            return carry

        lax.fori_loop(0, groups, body, 0, unroll=True)
        write(1, c, update.at[chunk_rows(c)], update_hbm.at[chunk_rows(c)])

    def momentum_chunk(c):
        for i in range(2):
            g_copies[c, i].wait_recv()

        def forward(g, carry):
            rows = pl.ds(pl.multiple_of(g * GROUP, GROUP), GROUP)
            moment = g_own[c, rows] + g_recv[c, rows].astype(F32)
            g_own[c, rows] = moment
            high, low = split(left_band(moment))
            packed[pl.ds(0, 64), group_lanes(g)] = jnp.concatenate([high, low], axis=1)
            return carry

        lax.fori_loop(0, groups, forward, 0, unroll=True)
        c_send_own = right_band(64)

        def back(g, carry):
            rows = pl.ds(pl.multiple_of(g * GROUP, GROUP), GROUP)
            new_mom[group_rows(c, g)] = (g_own[c, rows] - inverse(c_send_own, g)).astype(BF)
            return carry

        lax.fori_loop(0, groups, back, 0, unroll=True)
        write(0, c, new_mom.at[chunk_rows(c)], new_mom_hbm.at[chunk_rows(c)])

    def partial_half(c, i):
        if i == 1:
            for copy in to_core[c]:
                copy.wait_recv()
        which = core if i == 0 else 1 - core
        for j in range(groups // 2):
            g = which * (groups // 2) + j
            p = mm(k_rows[...].reshape(2 * TOK, 512), w_all[group_rows(c, g)], ((1,), (1,)))
            p_own[c, :, group_lanes(g)] = p[:TOK]
            p_send[c, :, group_lanes(g)] = p[TOK:].astype(BF)
        cols = pl.ds(pl.multiple_of(which * half, half), half)
        p_copies[c, i] = send(p_send.at[c, :, cols], p_recv.at[c, :, cols], ps.at[c, i], pr.at[c, i], device(yl=1 - yl))

    other_core = device(core=1 - core)
    for copy in local:
        copy.wait()

    def receive(s):
        for copy in first_hop[s]:
            copy.wait_recv()
        second_hop[s] = forward_item(s)

    def complete(s):
        for copy in second_hop[s]:
            copy.wait_recv()

    for h in range(HALVES):
        receive(h)
        if h + 3 < HALVES:
            first_hop[h + 3] = send_item(h + 3)
        if h == HALVES - 1:
            for c in range(2):
                first_hop[HALVES + c] = send_item(HALVES + c)
        if h == 1:
            for copy in k_copies:
                copy.wait_recv()
        if h >= 2:
            complete(h - 2)
            gradient_half(h - 2)
        if h < 3:
            pl.semaphore_wait(z_sem.at[h], 2)
            if h < 2:
                z_round(h + 1)
        if h in (5, 7):
            reduce_near(h // 2 - 2)
        if h == 7:
            momentum_chunk(0)
    for h in (HALVES - 2, HALVES - 1):
        complete(h)
        gradient_half(h)

    for w in range(CHUNKS + 2):
        if w < CHUNKS:
            receive(HALVES + w)
            if w + 2 < CHUNKS:
                first_hop[HALVES + w + 2] = send_item(HALVES + w + 2)
            to_core[w] = []
            for i, owner in enumerate((left, right)):
                piece = weight_piece(w, owner)
                to_core[w].append(send(piece, piece, cs.at[w, i], cr.at[w, i], other_core))
        if 1 <= w <= CHUNKS:
            complete(HALVES + w - 1)
            piece = weight_piece(w - 1, across)
            to_core[w - 1].append(send(piece, piece, cs.at[w - 1, 2], cr.at[w - 1, 2], other_core))
        if w >= 2:
            partial_half(w - 2, 1)
        if 1 <= w <= CHUNKS:
            partial_half(w - 1, 0)
        for act in LATE[w]:
            {"near": reduce_near, "far": reduce_far, "mom": momentum_chunk, "upd": update_chunk}[act[0]](act[1])

    for c in range(CHUNKS):
        for i in range(2):
            p_copies[c, i].wait_recv()
        in_grad[:, chunk_rows(c)] = (p_own[c] + p_recv[c].astype(F32)).astype(BF)
        write(2, c, in_grad.at[:, chunk_rows(c)], in_grad_hbm.at[:, chunk_rows(c)])

    for copy in written:
        copy.wait()
    for copy in sent:
        copy.wait_send()
    for c in range(CHUNKS):
        for copy in (s1_all(c), s2_all(c), s3_all(c)):
            copy.wait_send()


def hand_over(a, b, c, a_out, b_out, c_out, a_here, b_here, c_here, in_sem, out_sem):
    arrays = ((a, a_here, a_out), (b, b_here, b_out), (c, c_here, c_out))
    pieces = []
    for i, (src, here, dst) in enumerate(arrays):
        rows = src.shape[0] // 2
        for j in range(2):
            part = pl.ds(j * rows, rows)
            first = pltpu.make_async_copy(src.at[part], here.at[part], in_sem.at[i, j])
            second = pltpu.make_async_copy(here.at[part], dst.at[part], out_sem.at[i, j])
            first.start()
            pieces.append((first, second))
    for first, second in pieces:
        first.wait()
        second.start()
    for _, second in pieces:
        second.wait()


def cosine_table():
    freq = np.arange(SPAN, dtype=np.float64)[:, None]
    cell = np.arange(SPAN, dtype=np.float64)[None, :]
    scale = np.where(freq == 0.0, math.sqrt(1.0 / SPAN), math.sqrt(2.0 / SPAN))
    return (np.cos(math.pi * (2.0 * cell + 1.0) * freq / (2.0 * SPAN)) * scale).astype(np.float32)


def split_cosines():
    table = cosine_table()
    high = table.astype(BF)
    low = (table - high.astype(np.float32)).astype(BF)
    return np.stack([np.tile(high, (1, 4)), np.tile(low, (1, 4))])


def per_device(tokens, key_grad, key_weight, momentum, band_freqs):
    d_in = tokens.shape[1]
    width = d_in // CHUNKS
    vmem = pl.BlockSpec(memory_space=pltpu.VMEM)
    hbm = pl.BlockSpec(memory_space=pltpu.HBM)
    dma = pltpu.SemaphoreType.DMA
    new_momentum, update, input_grad = pl.pallas_call(
        kernel,
        out_shape=(
            jax.ShapeDtypeStruct((d_in, 128), BF),
            jax.ShapeDtypeStruct((d_in, 128), BF),
            jax.ShapeDtypeStruct((TOK, d_in), BF),
        ),
        in_specs=[hbm, hbm, hbm, hbm, vmem, vmem],
        out_specs=(hbm, hbm, hbm),
        scratch_shapes=[
            pltpu.VMEM((d_in, 128), BF),
            pltpu.VMEM((d_in, 128), BF),
            pltpu.VMEM((TOK, d_in), BF),
            pltpu.VMEM((d_in, 128), BF),
            pltpu.VMEM((128, GROUP), BF),
            pltpu.VMEM((4 * GROUP, 256), BF),
            pltpu.VMEM((128, 4 * GROUP), BF),
            pltpu.VMEM((GROUP, 256), BF),
            pltpu.VMEM((HALVES, N_X, TOK, width // 2), BF),
            pltpu.VMEM((N_X, TOK, 256), BF),
            pltpu.VMEM((2, TOK, 512), BF),
            pltpu.VMEM((d_in, 512), BF),
            pltpu.VMEM((CHUNKS, width, 128), F32),
            pltpu.VMEM((CHUNKS, width, 128), BF),
            pltpu.VMEM((CHUNKS, width, 128), BF),
            pltpu.VMEM((CHUNKS, 2, 64, 128), BF),
            pltpu.VMEM((CHUNKS, 8, BAND, 128), BF),
            pltpu.VMEM((CHUNKS, N_Z, BAND, 128), BF),
            pltpu.VMEM((CHUNKS, 64, 128), BF),
            pltpu.VMEM((128, 4 * GROUP), BF),
            pltpu.VMEM((CHUNKS, TOK, width), F32),
            pltpu.VMEM((CHUNKS, TOK, width), BF),
            pltpu.VMEM((CHUNKS, TOK, width), BF),
            dma((5 + HALVES,)),
            dma((7,)),
            dma((7,)),
            dma((HALVES, 4)),
            dma((HALVES, 4)),
            dma((CHUNKS, 4)),
            dma((CHUNKS, 4)),
            dma((CHUNKS, 3)),
            dma((CHUNKS, 3)),
            dma((CHUNKS, 2)),
            dma((CHUNKS, 2)),
            dma((CHUNKS, 2)),
            dma((CHUNKS, 2)),
            dma((CHUNKS,)),
            dma((CHUNKS,)),
            dma((CHUNKS,)),
            dma((CHUNKS,)),
            dma((CHUNKS,)),
            dma((CHUNKS,)),
            pltpu.SemaphoreType.REGULAR((3,)),
            dma((3, CHUNKS)),
        ],
        compiler_params=pltpu.CompilerParams(
            collective_id=0, has_side_effects=True, vmem_limit_bytes=62 << 20
        ),
        name="band_step",
    )(tokens, key_grad.reshape(N_X, 2 * TOK, 128), key_weight, momentum[0], band_freqs, split_cosines())
    outs = (new_momentum, update, input_grad)
    new_momentum, update, input_grad = pl.pallas_call(
        hand_over,
        out_shape=tuple(jax.ShapeDtypeStruct(o.shape, o.dtype) for o in outs),
        in_specs=[pl.BlockSpec(memory_space=pl.ANY)] * 3,
        out_specs=(hbm,) * 3,
        scratch_shapes=[pltpu.VMEM(o.shape, o.dtype) for o in outs] + [dma((3, 2)), dma((3, 2))],
        name="hand_over",
    )(*outs)
    return new_momentum[None], update, input_grad


def solution(mesh):
    placed = (P(("dp", "mp"), None), P("dp", "mp"), P(None, "mp"), P("dp", None, "mp"), P())
    return jax.shard_map(
        per_device,
        mesh=mesh,
        in_specs=placed,
        out_specs=(P("dp", None, "mp"), P(None, "mp"), P(("dp", "mp"), None)),
        check_vma=False,
    )
```
